32 devices in a mesh: tile: 8 (over z, y), head: 4 (over x, core).
Axes of the slice: x: 2, y: 2, z: 4, core: 2. Of those that a mesh axis runs over, the one named last changes fastest.
Arguments:
- latents: bfloat16 [7200, 5120], P('tile'), may hold values from -1000 to 1000
- query_weight: bfloat16 [5120, 2560], P('tile', 'head'), may hold values from -1.5 to 1.5
- mod_shift: float32 [5120], replicated, may hold values from -3 to 3
- mod_scale: float32 [5120], replicated, may hold values from -3 to 3
- query_gain: float32 [2560], P('head'), may hold values from 0.5 to 2
- cache_blocks: bfloat16 [7200, 2, 2560], P('tile', None, 'head'), may hold values from -640 to 640
- block_counts: int32 [8], replicated, may hold values from 1 to 900, 5400 in all
- group_index: int32 [1], replicated, may hold values from 1 to 20
Outputs:
- attended: bfloat16 [7200, 2560], P('tile', 'head')
The draws below stay inside these ranges and needn't reach their ends.
Inputs may be any that keep to these rules, and one draw needn't show every extreme that they name: `block_counts`: entry t counts the valid cached tokens of tile t; they are its first ones; the largest entry is exactly 900.
All inputs are finite; a program needn't handle non-finite values.
Results may differ from the reference program's by a relative error of at most 0.008.
The reference program's roundings to bfloat16 on the way count: a program that leaves them out, or rounds other values in their place, can miss the bound.
Values may be sent and summed in bfloat16 or wider, within the bound.
A program may use at most 128 MiB of HBM per device.

```python
import math
import jax
import jax.numpy as jnp
import numpy as np
from jax import lax

D = 5120
HEADS = 20
HD = 128
FRAMES = 3
GH = 45
GW = 80
CLIP_TOK = 3600
TPC = 4
TOK_DEV = 900
TOKENS = 7200
N_TILE = 8


def draw_latents(key, part):
    noise_key, row_key, col_key = jax.random.split(jax.random.fold_in(key, 11), 3)
    noise = jnp.clip(jax.random.normal(noise_key, (TOKENS, D), jnp.float32), -6.0, 6.0)
    row_scale = 10.0 ** jax.random.uniform(row_key, (TOKENS, 1), jnp.float32)
    col_scale = 10.0 ** jax.random.uniform(col_key, (1, D), jnp.float32)
    return (noise * row_scale * col_scale).astype(jnp.bfloat16)


def draw_query_weight(key, part):
    noise_key = jax.random.fold_in(key, 23)
    columns = HEADS * HD
    place = jnp.arange(columns, dtype=jnp.float32) / columns - 0.5
    noise = jnp.clip(jax.random.normal(noise_key, (D, columns), jnp.float32), -6.0, 6.0)
    col_scale = 10.0 ** place
    return (noise * col_scale[None, :] / jnp.sqrt(jnp.float32(D))).astype(jnp.bfloat16)


def draw_cache_blocks(key, part):
    key_key, value_key = jax.random.split(jax.random.fold_in(key, 37), 2)
    columns = HEADS * HD
    key_part = 1.5 * jnp.clip(jax.random.normal(key_key, (TOKENS, columns), jnp.float32), -6.0, 6.0)
    value_part = 3.0 * jnp.clip(jax.random.normal(value_key, (TOKENS, columns), jnp.float32), -4.0, 4.0)
    return jnp.stack([key_part, value_part], axis=1).astype(jnp.bfloat16)


def level_of(rng, dims, cuts, low, high):
    level = 1.0
    for dim, shards_of in cuts:
        draws = jax.random.uniform(jax.random.fold_in(jax.random.fold_in(rng, 6), dim), (shards_of,), jnp.float32, low / len(cuts), high / len(cuts))
        level = level * jnp.repeat(jnp.exp(draws), dims[dim] // shards_of).reshape((-1,) + (1,) * (len(dims) - 1 - dim))
    return level


def length_profile(count, total, reach, slope):
    portions = [(1 << 20) // math.isqrt(rank ** slope) + 1 for rank in range(2, count + 1)]
    rest, given = total - reach - (count - 1), [1] * (count - 1)
    while rest > 0:
        movable = [i for i in range(count - 1) if given[i] < reach]
        mass, budget = sum([portions[i] for i in movable]), rest
        for i in movable:
            more = min(reach - given[i], max(1, budget * portions[i] // mass), rest)
            given[i] = given[i] + more
            rest = rest - more
    return np.array([reach] + given)


def uneven(stream_key, number_of, total, reach, slope):
    if number_of == 2:
        one = jax.random.randint(stream_key, (), max(1, total - reach), min(reach, total - 1) + 1)
        return jnp.stack([one, total - one])
    lengths = jnp.asarray(length_profile(number_of, total, reach, slope), jnp.int32)
    couples = (number_of - 1) // 2
    giver, taker = lengths[1:1 + 2 * couples:2], lengths[2:2 + 2 * couples:2]
    slack = jnp.minimum(giver - 1, reach - taker)
    moved = jax.random.randint(jax.random.fold_in(stream_key, 1), (couples,), 0, 1 << 20) % (slack + 1)
    lengths = lengths.at[1:1 + 2 * couples:2].set(giver - moved).at[2:2 + 2 * couples:2].set(taker + moved)
    return lengths[jax.random.permutation(jax.random.fold_in(stream_key, 2), number_of)]


def centred(stream_key, shape, width, most, kind=jnp.bfloat16):
    array = width * jax.random.normal(stream_key, shape, jnp.float32)
    return jnp.clip(array, min=-most, max=most).astype(kind)


def setup_inputs(seed: int = 0) -> dict:
    key_of = jax.random.split(jax.random.key(seed), 9)
    return {
        "latents": draw_latents(jax.random.fold_in(key_of[8], 71), 0),
        "query_weight": draw_query_weight(jax.random.fold_in(key_of[8], 71), 0),
        "mod_shift": centred(key_of[2], (D,), 0.5, 3.0, jnp.float32),
        "mod_scale": centred(key_of[3], (D,), 0.5, 3.0, jnp.float32),
        "query_gain": jnp.clip(jnp.exp(math.log(2.0) - 1.3862944 * jax.random.uniform(key_of[4], (HEADS * HD,), jnp.float32) ** level_of(key_of[4], (HEADS * HD,), ((0, 4),), -0.2, 0.2)), 0.5, 2.0),
        "cache_blocks": draw_cache_blocks(jax.random.fold_in(key_of[8], 71), 0),
        "block_counts": uneven(key_of[6], N_TILE, N_TILE * TOK_DEV * 3 // 4, TOK_DEV, 1).astype(jnp.int32),
        "group_index": jax.random.randint(key_of[7], (1,), 1, 21).astype(jnp.int32),
    }


norm_eps = 1e-06

def rotary_tables(place_index, group_value, token_count, head_dim):
    local = place_index * token_count + jnp.arange(token_count, dtype=jnp.int32)
    frame_pos = local // (GH * GW)
    row_pos = local // GW % GH
    col_pos = local % GW
    time_pos = (group_value * FRAMES + frame_pos).astype(jnp.float32)
    height_pos = row_pos.astype(jnp.float32)
    width_pos = col_pos.astype(jnp.float32)
    half_dim = head_dim // 2
    space_pairs = head_dim // 6
    time_pairs = half_dim - 2 * space_pairs
    pair_index = jnp.arange(half_dim, dtype=jnp.int32)
    in_time = pair_index < time_pairs
    in_height = pair_index < time_pairs + space_pairs
    offset = jnp.where(in_time, pair_index, jnp.where(in_height, pair_index - time_pairs, pair_index - time_pairs - space_pairs))
    extent = jnp.where(in_time, time_pairs, space_pairs)
    theta = jnp.exp(-math.log(10000.0) * offset.astype(jnp.float32) / extent.astype(jnp.float32))
    position = jnp.where(in_time[None, :], time_pos[:, None], jnp.where(in_height[None, :], height_pos[:, None], width_pos[:, None]))
    angle = position * theta[None, :]
    return (jnp.cos(angle), jnp.sin(angle))

def rotate_pairs(scaled, cos_table, sin_table):
    token_count, head_count, head_dim = scaled.shape
    paired = scaled.reshape(token_count, head_count, head_dim // 2, 2)
    first_part = paired[..., 0]
    second_part = paired[..., 1]
    cos_wide = cos_table[:, None, :]
    sin_wide = sin_table[:, None, :]
    turned = jnp.stack([first_part * cos_wide - second_part * sin_wide, first_part * sin_wide + second_part * cos_wide], axis=-1)
    return turned.reshape(token_count, head_count, head_dim)

def reference(latents, query_weight, mod_shift, mod_scale, query_gain, cache_blocks, block_counts, group_index):
    tiled = latents.reshape(N_TILE, TOK_DEV, D)
    slot_numbers = jnp.arange(CLIP_TOK, dtype=jnp.int32)
    slot_tile = slot_numbers // TOK_DEV
    slot_local = slot_numbers % TOK_DEV

    def one_tile(item):
        tile_index, tile_rows = item
        clip_start = tile_index // TPC * TPC
        widened = tile_rows.astype(jnp.float32)
        row_mean = lax.optimization_barrier(jnp.sum(widened, axis=1, keepdims=True)) / D
        row_var = lax.optimization_barrier(jnp.sum(widened * widened, axis=1, keepdims=True)) / D - row_mean * row_mean
        normed = ((widened - row_mean) * lax.rsqrt(row_var + norm_eps) * (1.0 + mod_scale) + mod_shift).astype(jnp.bfloat16)
        queries = jnp.dot(normed, query_weight, preferred_element_type=jnp.float32)
        squares = lax.optimization_barrier(jnp.sum(queries * queries, axis=1, keepdims=True)) / (HEADS * HD)
        scaled = queries * lax.rsqrt(squares + norm_eps) * query_gain
        cos_table, sin_table = rotary_tables(tile_index % TPC, group_index[0], TOK_DEV, HD)
        rotated = rotate_pairs(scaled.reshape(TOK_DEV, HEADS, HD), cos_table, sin_table).astype(jnp.bfloat16)
        clip_cache = lax.dynamic_slice_in_dim(cache_blocks, (clip_start * TOK_DEV).astype(jnp.int32), CLIP_TOK, 0)
        cached_keys = clip_cache[:, 0, :].reshape(CLIP_TOK, HEADS, HD).astype(jnp.float32)
        cached_values = clip_cache[:, 1, :].reshape(CLIP_TOK, HEADS, HD).astype(jnp.float32)
        counts_clip = lax.dynamic_slice_in_dim(block_counts, clip_start.astype(jnp.int32), TPC)
        valid_mask = slot_local < counts_clip[slot_tile]
        scores = jnp.einsum('thd,khd->htk', rotated.astype(jnp.float32), cached_keys) * (1.0 / math.sqrt(HD))
        masked = jnp.where(valid_mask[None, None, :], scores, -1e+30)
        top_score = lax.optimization_barrier(jnp.max(masked, axis=2, keepdims=True))
        weights = jnp.where(valid_mask[None, None, :], jnp.exp(masked - top_score), 0.0)
        totals = lax.optimization_barrier(jnp.sum(weights, axis=2))
        rounded = weights.astype(jnp.bfloat16)
        mixed = jnp.einsum('htk,khd->thd', rounded.astype(jnp.float32), cached_values)
        attended = (mixed / jnp.transpose(totals)[:, :, None]).astype(jnp.bfloat16)
        return attended.reshape(TOK_DEV, HEADS * HD)
    outputs = lax.map(one_tile, (jnp.arange(N_TILE, dtype=jnp.int32), tiled))
    return outputs.reshape(TOKENS, HEADS * HD)
```

```python
import functools
import math

import jax
import jax.numpy as jnp
import numpy as np
from jax import lax
from jax.experimental import pallas as pl
from jax.experimental.pallas import tpu as pltpu
from jax.sharding import PartitionSpec as P

D = 5120
HEADS = 20
HD = 128
FRAMES = 3
WINDOW = 1
GH = 45
GW = 80


norm_eps = 1e-06


def from_partner(value, axis, stride):
    mask = 2**stride
    pairs = [(source, source ^ mask) for source in range(lax.axis_size(axis))]
    return lax.ppermute(value, axis, pairs)


def rotary_tables(place_index, group_value, token_count, head_dim):
    local = place_index * token_count + jnp.arange(token_count, dtype=jnp.int32)
    frame_pos = local // (GH * GW)
    row_pos = local // GW % GH
    col_pos = local % GW
    time_pos = (group_value * FRAMES + frame_pos).astype(jnp.float32)
    height_pos = row_pos.astype(jnp.float32)
    width_pos = col_pos.astype(jnp.float32)
    half_dim = head_dim // 2
    space_pairs = head_dim // 6
    time_pairs = half_dim - 2 * space_pairs
    pair_index = jnp.arange(half_dim, dtype=jnp.int32)
    in_time = pair_index < time_pairs
    in_height = pair_index < time_pairs + space_pairs
    offset = jnp.where(
        in_time,
        pair_index,
        jnp.where(in_height, pair_index - time_pairs, pair_index - time_pairs - space_pairs),
    )
    extent = jnp.where(in_time, time_pairs, space_pairs)
    theta = jnp.exp(-math.log(10000.0) * offset.astype(jnp.float32) / extent.astype(jnp.float32))
    position = jnp.where(
        in_time[None, :],
        time_pos[:, None],
        jnp.where(in_height[None, :], height_pos[:, None], width_pos[:, None]),
    )
    angle = position * theta[None, :]
    return (jnp.cos(angle), jnp.sin(angle))


def rotate_pairs(scaled, cos_table, sin_table):
    token_count, head_count, head_dim = scaled.shape
    paired = scaled.reshape(token_count, head_count, head_dim // 2, 2)
    first_part = paired[..., 0]
    second_part = paired[..., 1]
    cos_wide = cos_table[:, None, :]
    sin_wide = sin_table[:, None, :]
    turned = jnp.stack(
        [
            first_part * cos_wide - second_part * sin_wide,
            first_part * sin_wide + second_part * cos_wide,
        ],
        axis=-1,
    )
    return turned.reshape(token_count, head_count, head_dim)


def per_device(
    latents, query_weight, mod_shift, mod_scale, query_gain, cache_blocks, block_counts, group_index
):
    token_count = latents.shape[0]
    width_here = query_weight.shape[1]
    heads_here = width_here // HD
    widened = latents.astype(jnp.float32)
    row_mean = jnp.sum(widened, axis=1, keepdims=True) / D
    row_var = jnp.sum(widened * widened, axis=1, keepdims=True) / D - row_mean * row_mean
    normed = (
        (widened - row_mean) * lax.rsqrt(row_var + norm_eps) * (1.0 + mod_scale) + mod_shift
    ).astype(jnp.bfloat16)
    queries = jnp.dot(
        normed,
        lax.all_gather(query_weight, "tile", axis=0, tiled=True),
        preferred_element_type=jnp.float32,
    )
    squares = lax.psum(jnp.sum(queries * queries, axis=1), "head")
    scaled = queries * lax.rsqrt(squares[:, None] / (HEADS * HD) + norm_eps) * query_gain
    clip_span = WINDOW * GH * GW // token_count
    tile_index = lax.axis_index("tile")
    place_index = tile_index % clip_span
    cos_table, sin_table = rotary_tables(place_index, group_index[0], token_count, HD)
    rotated = rotate_pairs(
        scaled.reshape(token_count, heads_here, HD), cos_table, sin_table
    ).astype(jnp.bfloat16)
    rotated_flat = rotated.reshape(token_count, width_here)
    bit_total = clip_span.bit_length() - 1
    bit_sequence = list(range(bit_total))
    cache_rows = cache_blocks
    slot_order = np.zeros(1, np.int32)
    for bit_number in bit_sequence:
        partner = from_partner(cache_rows, "tile", bit_number)
        mine_high = tile_index >> bit_number & 1 == 1
        lower_rows = jnp.where(mine_high, partner, cache_rows)
        upper_rows = jnp.where(mine_high, cache_rows, partner)
        cache_rows = jnp.concatenate([lower_rows, upper_rows], axis=0)
        slot_order = np.concatenate([slot_order, slot_order + (1 << bit_number)])
    clip_base = tile_index - place_index
    counts_here = lax.dynamic_slice_in_dim(block_counts, clip_base, clip_span)
    order_table = jnp.asarray(slot_order, jnp.int32)
    span_numbers = jnp.arange(clip_span, dtype=jnp.int32)
    counts_ordered = jnp.sum(
        jnp.where(span_numbers[None, :] == order_table[:, None], counts_here[None, :], 0), axis=1
    )
    valid_mask = (
        jnp.arange(token_count, dtype=jnp.int32)[None, :] < counts_ordered[:, None]
    ).reshape(-1)
    keys_all = cache_rows[:, 0, :]
    values_all = cache_rows[:, 1, :]
    score_scale = 1.0 / math.sqrt(HD)

    def one_head(head_number):
        first_col = head_number * HD
        query_part = lax.dynamic_slice_in_dim(rotated_flat, first_col, HD, 1)
        key_part = lax.dynamic_slice_in_dim(keys_all, first_col, HD, 1)
        value_part = lax.dynamic_slice_in_dim(values_all, first_col, HD, 1)
        scores = (
            lax.dot_general(
                query_part, key_part, (((1,), (1,)), ((), ())), preferred_element_type=jnp.float32
            )
            * score_scale
        )
        masked = jnp.where(valid_mask[None, :], scores, -1e30)
        top_score = jnp.max(masked, axis=1, keepdims=True)
        weights = jnp.where(valid_mask[None, :], jnp.exp(masked - top_score), 0.0)
        totals = jnp.sum(weights, axis=1, keepdims=True)
        rounded = weights.astype(jnp.bfloat16)
        mixed = jnp.dot(rounded, value_part, preferred_element_type=jnp.float32)
        return (mixed / totals).astype(jnp.bfloat16)

    per_head = lax.map(one_head, jnp.arange(heads_here, dtype=jnp.int32))
    return jnp.transpose(per_head, (1, 0, 2)).reshape(token_count, width_here)


MESH = pl.DeviceIdType.MESH
LANES = 128
Z_ORDER = ((0, 1, 2, 3), (1, 0, 2, 3), (2, 3, 1, 0), (3, 2, 1, 0))
STEPS = ((0, 1), (1, 1), (0, 0), (2, 1), (1, 0), (3, 1), (2, 0), (3, 0))


def pick(index, values):
    out = jnp.int32(values[-1])
    for place in range(len(values) - 1):
        out = jnp.where(index == place, jnp.int32(values[place]), out)
    return out


def project_kernel(
    lat_ref, w_ref, shift_ref, scale_ref, gain_ref, k_ref, v_ref, group_ref,
    q_ref, k_all, v_all,
    lat, wbuf, acc, part, mean_s, rstd_s, cos_s, sin_s, rot, sq,
    lat_sem, w_local, w_recv, w_sendy, w_sendr, w_sendl,
    sq_recv, sq_send, q_send, q_recv, kv_recv, kv_y, kv_z, kv_relay, kv_sib,
):
    tile = lax.axis_index("tile")
    head = lax.axis_index("head")
    z, y = tile // 2, tile % 2
    core = head % 2
    zlow = z % 2
    tile_y = z * 2 + (1 - y)
    head_sib = head - core + (1 - core)
    zpair = z - zlow + (1 - zlow)
    tile_zp = zpair * 2 + y
    own = zlow * 2 + y
    own_y = zlow * 2 + (1 - y)
    far = (1 - zlow) * 2 + y
    far_y = (1 - zlow) * 2 + (1 - y)
    rows = lat.shape[0]
    depth = w_ref.shape[0]
    is_main = core == y
    not_main = core != y
    heads_here = acc.shape[1] // LANES

    def remote(src, dst, ssem, rsem, tile_to, head_to):
        return pltpu.make_async_remote_copy(
            src_ref=src, dst_ref=dst, send_sem=ssem, recv_sem=rsem,
            device_id=(tile_to, head_to), device_id_type=MESH,
        )

    def greet(tile_to, head_to):
        pl.semaphore_signal(
            barrier, inc=1, device_id=(tile_to, head_to), device_id_type=MESH
        )

    barrier = pltpu.get_barrier_semaphore()
    greet(tile_y, head)
    greet(tile_y, head_sib)
    for other in range(1, 4):
        greet(tile, (head + other) % 4)
    pl.when(z > 0)(lambda: greet(tile - 2, head))
    pl.when(z < 3)(lambda: greet(tile + 2, head))
    lat_copy = pltpu.make_async_copy(lat_ref, lat, lat_sem)
    lat_copy.start()
    w_copy = pltpu.make_async_copy(w_ref, wbuf.at[tile], w_local)
    w_copy.start()
    pl.semaphore_wait(barrier, 5 + pick(z, (1, 2, 2, 1)))

    def send_y(zk):
        slot = zk * 2 + y
        return remote(wbuf.at[slot], wbuf.at[slot], w_sendy.at[zk], w_recv.at[slot], tile_y, head)

    def send_right(zk):
        slot = zk * 2 + y
        return remote(wbuf.at[slot], wbuf.at[slot], w_sendr.at[zk], w_recv.at[slot], tile + 2, head)

    def send_left(zk):
        slot = zk * 2 + y
        return remote(wbuf.at[slot], wbuf.at[slot], w_sendl.at[zk], w_recv.at[slot], tile - 2, head)

    def forward(zk):
        pl.when(jnp.logical_and(zk <= z, z < 3))(lambda: send_right(zk).start())
        pl.when(jnp.logical_and(zk >= z, z > 0))(lambda: send_left(zk).start())
        send_y(zk).start()

    kv = ((k_ref, k_all), (v_ref, v_all))

    def kv_local(i):
        return pltpu.make_async_copy(kv[i][0], kv[i][1].at[own], kv_recv.at[i, own])

    def kv_to_y(i):
        return remote(kv[i][0], kv[i][1].at[own], kv_y.at[i], kv_recv.at[i, own], tile_y, head)

    def kv_to_z(i):
        return remote(kv[i][0], kv[i][1].at[own], kv_z.at[i], kv_recv.at[i, own], tile_zp, head)

    def kv_to_relay(i):
        return remote(
            kv[i][1].at[own_y], kv[i][1].at[own_y], kv_relay.at[i], kv_recv.at[i, own_y],
            tile_zp, head,
        )

    def kv_to_sib(i, slot):
        src = kv[i][0] if slot is own else kv[i][1].at[slot]
        return remote(
            src, kv[i][1].at[slot], kv_sib.at[i, slot], kv_recv.at[i, slot], tile, head_sib
        )

    def kv_wait(i, slot):
        remote(
            kv[i][1].at[slot], kv[i][1].at[slot], kv_sib.at[i, slot], kv_recv.at[i, slot],
            tile, head_sib,
        ).wait_recv()

    w_copy.wait()
    forward(z)
    lat_copy.wait()

    part[...] = jnp.zeros_like(part)
    acc[:, :LANES] = jnp.zeros_like(part)

    def columns(i):
        return pl.ds(pl.multiple_of(i * LANES, LANES), LANES)

    @pl.loop(0, D // LANES)
    def _(i):
        x = lat[:, columns(i)].astype(jnp.float32)
        part[...] += x
        acc[:, :LANES] += x * x

    mean = jnp.sum(part[...], axis=1, keepdims=True) / D
    var = jnp.sum(acc[:, :LANES], axis=1, keepdims=True) / D - mean * mean
    mean_s[...] = jnp.broadcast_to(mean, mean_s.shape)
    rstd_s[...] = jnp.broadcast_to(lax.rsqrt(var + norm_eps), rstd_s.shape)

    @pl.loop(0, D // LANES)
    def _(i):
        x = lat[:, columns(i)].astype(jnp.float32)
        normed = (x - mean_s[...]) * rstd_s[...] * (1.0 + scale_ref[:, columns(i)])
        lat[:, columns(i)] = (normed + shift_ref[:, columns(i)]).astype(jnp.bfloat16)

    lane = lax.broadcasted_iota(jnp.int32, (1, LANES), 1)
    pair = lane // 2
    space_pairs = HD // 6
    time_pairs = HD // 2 - 2 * space_pairs
    in_time = pair < time_pairs
    in_height = pair < time_pairs + space_pairs
    offset = jnp.where(
        in_time, pair, jnp.where(in_height, pair - time_pairs, pair - time_pairs - space_pairs)
    )
    extent = jnp.where(in_time, jnp.float32(time_pairs), jnp.float32(space_pairs))
    theta = jnp.exp(-math.log(10000.0) * offset.astype(jnp.float32) / extent)
    token = (
        own * rows + lax.broadcasted_iota(jnp.int32, (rows, LANES), 0)
    ).astype(jnp.float32)
    frame = jnp.floor((token + 0.5) * (1.0 / (GH * GW)))
    in_frame = token - frame * (GH * GW)
    height = jnp.floor((in_frame + 0.5) * (1.0 / GW))
    width = in_frame - height * GW
    time = (group_ref[0] * FRAMES).astype(jnp.float32) + frame
    position = jnp.where(in_time, time, jnp.where(in_height, height, width))
    angle = position * theta
    even = lane % 2 == 0
    cos_s[...] = jnp.cos(angle)
    sine = jnp.sin(angle)
    sin_s[...] = jnp.where(even, -sine, sine)

    acc[...] = jnp.zeros_like(acc)

    @pl.loop(0, 8)
    def _(e):
        k = pick(e, [s[0] for s in STEPS])
        along_z = pick(e, [s[1] for s in STEPS])
        zk = jnp.where(
            z == 0, pick(k, Z_ORDER[0]),
            jnp.where(z == 1, pick(k, Z_ORDER[1]),
                      jnp.where(z == 2, pick(k, Z_ORDER[2]), pick(k, Z_ORDER[3]))),
        )
        slot = zk * 2 + jnp.where(along_z == 1, y, 1 - y)

        @pl.when(e > 0)
        def _():
            remote(
                wbuf.at[slot], wbuf.at[slot], w_sendy.at[zk], w_recv.at[slot], tile_y, head
            ).wait_recv()

        @pl.when(jnp.logical_and(e > 0, along_z == 1))
        def _():
            forward(zk)

        @pl.when(e == 5)
        def _():
            @pl.when(is_main)
            def _():
                for i in range(2):
                    kv_to_z(i).start()
                    kv_local(i).start()
                    kv_to_sib(i, own).start()

            @pl.when(not_main)
            def _():
                for i in range(2):
                    kv_to_y(i).start()

        cols = pl.ds(pl.multiple_of(slot * depth, LANES), depth)
        acc[...] += jnp.dot(lat[:, cols], wbuf[slot], preferred_element_type=jnp.float32)

    total = jnp.zeros((rows, LANES), jnp.float32)
    for h in range(heads_here):
        x = acc[:, h * LANES:(h + 1) * LANES]
        total = total + x * x
    part[...] = total
    sq[head] = lax.dot_general(
        jnp.ones((8, LANES), jnp.float32), part[...], (((1,), (1,)), ((), ())),
        preferred_element_type=jnp.float32, precision=lax.Precision.HIGHEST,
    )

    def sq_copy(other, slot):
        return remote(
            sq.at[slot], sq.at[slot], sq_send.at[other - 1], sq_recv.at[slot],
            tile, (head + other) % 4,
        )

    for other in range(1, 4):
        sq_copy(other, head).start()
    for other in range(1, 4):
        sq_copy(other, (head + other) % 4).wait_recv()
    for other in range(1, 4):
        sq_copy(other, head).wait_send()
    summed = sq[0] + sq[1] + sq[2] + sq[3]
    first = (lax.broadcasted_iota(jnp.int32, (8, LANES), 0) == 0).astype(jnp.float32)
    spread = lax.dot_general(
        summed, first, (((0,), (0,)), ((), ())),
        preferred_element_type=jnp.float32, precision=lax.Precision.HIGHEST,
    )
    rstd_s[...] = lax.rsqrt(spread / (HEADS * HD) + norm_eps)
    for h in range(heads_here):
        cut = slice(h * LANES, (h + 1) * LANES)
        x = acc[:, cut] * rstd_s[...] * gain_ref[:, cut]
        turned = jnp.where(
            even, pltpu.roll(x, LANES - 1, 1), pltpu.roll(x, 1, 1)
        )
        rot[:, cut] = (x * cos_s[...] + turned * sin_s[...]).astype(jnp.bfloat16)

    def q_out():
        return remote(rot, q_ref, q_send, q_recv, tile_y, head_sib)

    def q_stay():
        return pltpu.make_async_copy(rot, q_ref, q_recv)

    pl.when(not_main)(lambda: q_out().start())
    pl.when(is_main)(lambda: q_stay().start())

    @pl.when(is_main)
    def _():
        for i in range(2):
            kv_wait(i, own_y)
            kv_to_relay(i).start()
            kv_to_sib(i, own_y).start()
        for i in range(2):
            kv_wait(i, far)
            kv_to_sib(i, far).start()
        for i in range(2):
            kv_wait(i, far_y)
            kv_to_sib(i, far_y).start()
        for i in range(2):
            kv_local(i).wait()
            kv_to_z(i).wait_send()
            kv_to_relay(i).wait_send()
            for slot in (own, own_y, far, far_y):
                kv_to_sib(i, slot).wait_send()
        q_stay().wait()

    @pl.when(not_main)
    def _():
        for i in range(2):
            kv_to_y(i).wait_send()
            for slot in (own, own_y, far, far_y):
                kv_wait(i, slot)
        q_out().wait_send()
        q_out().wait_recv()

    for zk in range(4):
        send_y(zk).wait_send()
        pl.when(jnp.logical_and(zk <= z, z < 3))(lambda: send_right(zk).wait_send())
        pl.when(jnp.logical_and(zk >= z, z > 0))(lambda: send_left(zk).wait_send())


def project(latents, query_weight, mod_shift, mod_scale, query_gain, keys, values, group_index):
    rows, width = latents.shape[0], query_weight.shape[1]
    any_spec = pl.BlockSpec(memory_space=pl.ANY)
    vmem = pl.BlockSpec(memory_space=pltpu.VMEM)
    dma = pltpu.SemaphoreType.DMA
    wide = pltpu.VMEM((rows, LANES), jnp.float32)
    return pl.pallas_call(
        project_kernel,
        out_shape=(
            jax.ShapeDtypeStruct((rows, width), jnp.bfloat16),
            jax.ShapeDtypeStruct((4, rows, width), jnp.bfloat16),
            jax.ShapeDtypeStruct((4, rows, width), jnp.bfloat16),
        ),
        in_specs=[
            any_spec, any_spec, vmem, vmem, vmem, any_spec, any_spec,
            pl.BlockSpec(memory_space=pltpu.SMEM),
        ],
        out_specs=(any_spec, any_spec, any_spec),
        scratch_shapes=[
            pltpu.VMEM((rows, D), jnp.bfloat16),
            pltpu.VMEM((8,) + query_weight.shape, jnp.bfloat16),
            pltpu.VMEM((rows, width), jnp.float32),
            wide, wide, wide, wide, wide,
            pltpu.VMEM((rows, width), jnp.bfloat16),
            pltpu.VMEM((4, 8, rows), jnp.float32),
            dma(()), dma(()), dma((8,)), dma((4,)), dma((4,)), dma((4,)),
            dma((4,)), dma((3,)), dma(()), dma(()),
            dma((2, 4)), dma((2,)), dma((2,)), dma((2,)), dma((2, 4)),
        ],
        compiler_params=pltpu.CompilerParams(
            collective_id=0, has_side_effects=True, vmem_limit_bytes=60 * 2**20
        ),
    )(
        latents, query_weight, mod_shift[None], mod_scale[None], query_gain[None],
        keys, values, group_index,
    )


def attend_kernel(counts_ref, q_ref, k_ref, v_ref, o_ref):
    span, slots = k_ref.shape[0], k_ref.shape[1]
    factor = math.log2(math.e) / math.sqrt(HD)
    query = q_ref[...]
    place = lax.broadcasted_iota(jnp.int32, (1, slots), 1)
    scores = []
    for j in range(span):
        raw = lax.dot_general(
            query, k_ref[j], (((1,), (1,)), ((), ())), preferred_element_type=jnp.float32
        )
        scores.append(jnp.where(place < counts_ref[j], raw, -1e30))
    top = functools.reduce(
        jnp.maximum, [jnp.max(s, axis=1, keepdims=True) for s in scores]
    )
    totals = jnp.zeros_like(top)
    mixed = jnp.zeros(o_ref.shape, jnp.float32)
    for j in range(span):
        weights = jnp.exp2((scores[j] - top) * factor)
        totals += jnp.sum(weights, axis=1, keepdims=True)
        mixed += jnp.dot(
            weights.astype(jnp.bfloat16), v_ref[j], preferred_element_type=jnp.float32
        )
    o_ref[...] = (mixed / totals).astype(jnp.bfloat16)


def attend(counts, queries, keys, values):
    rows, width = queries.shape
    span = keys.shape[0]
    block = 304
    whole = pl.BlockSpec((span, rows, HD), lambda h, i: (0, 0, h))
    return pl.pallas_call(
        attend_kernel,
        grid=(width // HD, pl.cdiv(rows, block)),
        out_shape=jax.ShapeDtypeStruct((rows, width), jnp.bfloat16),
        in_specs=[
            pl.BlockSpec(memory_space=pltpu.SMEM),
            pl.BlockSpec((block, HD), lambda h, i: (i, h)),
            whole, whole,
        ],
        out_specs=pl.BlockSpec((block, HD), lambda h, i: (i, h)),
        compiler_params=pltpu.CompilerParams(vmem_limit_bytes=48 * 2**20),
    )(counts, queries, keys, values)


def swap_pairs():
    pairs = []
    for tile in range(8):
        for head in range(4):
            here = tile * 4 + head
            there = here if tile % 2 == head % 2 else (tile ^ 1) * 4 + (head ^ 1)
            pairs.append((here, there))
    return pairs


def per_device_square(
    latents, query_weight, mod_shift, mod_scale, query_gain, cache_blocks, block_counts, group_index
):
    keys, values = cache_blocks[:, 0, :], cache_blocks[:, 1, :]
    queries, keys_all, values_all = project(
        latents, query_weight, mod_shift, mod_scale, query_gain, keys, values, group_index
    )
    counts = lax.dynamic_slice_in_dim(block_counts, lax.axis_index("tile") // 4 * 4, 4)
    attended = attend(counts, queries, keys_all, values_all)
    return lax.ppermute(attended, ("tile", "head"), swap_pairs())


def solution(mesh):
    in_specs = (
        P("tile", None),
        P("tile", "head"),
        P(),
        P(),
        P("head"),
        P("tile", None, "head"),
        P(),
        P(),
    )
    out_specs = P("tile", "head")
    square = mesh.shape["tile"] == 8 and mesh.shape["head"] == 4
    return jax.shard_map(
        per_device_square if square else per_device, mesh=mesh,
        in_specs=in_specs,
        out_specs=out_specs,
        check_vma=False,
    )
```

```python
import math

import jax
import jax.numpy as jnp
import numpy as np
from jax import lax
from jax.experimental import pallas as pl
from jax.experimental.pallas import tpu as pltpu
from jax.sharding import PartitionSpec as P

D = 5120
HEADS = 20
HD = 128
FRAMES = 3
WINDOW = 1
GH = 45
GW = 80


norm_eps = 1e-06


def from_partner(value, axis, stride):
    mask = 2**stride
    pairs = [(source, source ^ mask) for source in range(lax.axis_size(axis))]
    return lax.ppermute(value, axis, pairs)


def rotary_tables(place_index, group_value, token_count, head_dim):
    local = place_index * token_count + jnp.arange(token_count, dtype=jnp.int32)
    frame_pos = local // (GH * GW)
    row_pos = local // GW % GH
    col_pos = local % GW
    time_pos = (group_value * FRAMES + frame_pos).astype(jnp.float32)
    height_pos = row_pos.astype(jnp.float32)
    width_pos = col_pos.astype(jnp.float32)
    half_dim = head_dim // 2
    space_pairs = head_dim // 6
    time_pairs = half_dim - 2 * space_pairs
    pair_index = jnp.arange(half_dim, dtype=jnp.int32)
    in_time = pair_index < time_pairs
    in_height = pair_index < time_pairs + space_pairs
    offset = jnp.where(
        in_time,
        pair_index,
        jnp.where(in_height, pair_index - time_pairs, pair_index - time_pairs - space_pairs),
    )
    extent = jnp.where(in_time, time_pairs, space_pairs)
    theta = jnp.exp(-math.log(10000.0) * offset.astype(jnp.float32) / extent.astype(jnp.float32))
    position = jnp.where(
        in_time[None, :],
        time_pos[:, None],
        jnp.where(in_height[None, :], height_pos[:, None], width_pos[:, None]),
    )
    angle = position * theta[None, :]
    return (jnp.cos(angle), jnp.sin(angle))


def rotate_pairs(scaled, cos_table, sin_table):
    token_count, head_count, head_dim = scaled.shape
    paired = scaled.reshape(token_count, head_count, head_dim // 2, 2)
    first_part = paired[..., 0]
    second_part = paired[..., 1]
    cos_wide = cos_table[:, None, :]
    sin_wide = sin_table[:, None, :]
    turned = jnp.stack(
        [
            first_part * cos_wide - second_part * sin_wide,
            first_part * sin_wide + second_part * cos_wide,
        ],
        axis=-1,
    )
    return turned.reshape(token_count, head_count, head_dim)


def per_device(
    latents, query_weight, mod_shift, mod_scale, query_gain, cache_blocks, block_counts, group_index
):
    token_count = latents.shape[0]
    width_here = query_weight.shape[1]
    heads_here = width_here // HD
    widened = latents.astype(jnp.float32)
    row_mean = jnp.sum(widened, axis=1, keepdims=True) / D
    row_var = jnp.sum(widened * widened, axis=1, keepdims=True) / D - row_mean * row_mean
    normed = (
        (widened - row_mean) * lax.rsqrt(row_var + norm_eps) * (1.0 + mod_scale) + mod_shift
    ).astype(jnp.bfloat16)
    queries = jnp.dot(
        normed,
        lax.all_gather(query_weight, "tile", axis=0, tiled=True),
        preferred_element_type=jnp.float32,
    )
    squares = lax.psum(jnp.sum(queries * queries, axis=1), "head")
    scaled = queries * lax.rsqrt(squares[:, None] / (HEADS * HD) + norm_eps) * query_gain
    clip_span = WINDOW * GH * GW // token_count
    tile_index = lax.axis_index("tile")
    place_index = tile_index % clip_span
    cos_table, sin_table = rotary_tables(place_index, group_index[0], token_count, HD)
    rotated = rotate_pairs(
        scaled.reshape(token_count, heads_here, HD), cos_table, sin_table
    ).astype(jnp.bfloat16)
    rotated_flat = rotated.reshape(token_count, width_here)
    bit_total = clip_span.bit_length() - 1
    bit_sequence = list(range(bit_total))
    cache_rows = cache_blocks
    slot_order = np.zeros(1, np.int32)
    for bit_number in bit_sequence:
        partner = from_partner(cache_rows, "tile", bit_number)
        mine_high = tile_index >> bit_number & 1 == 1
        lower_rows = jnp.where(mine_high, partner, cache_rows)
        upper_rows = jnp.where(mine_high, cache_rows, partner)
        cache_rows = jnp.concatenate([lower_rows, upper_rows], axis=0)
        slot_order = np.concatenate([slot_order, slot_order + (1 << bit_number)])
    clip_base = tile_index - place_index
    counts_here = lax.dynamic_slice_in_dim(block_counts, clip_base, clip_span)
    order_table = jnp.asarray(slot_order, jnp.int32)
    span_numbers = jnp.arange(clip_span, dtype=jnp.int32)
    counts_ordered = jnp.sum(
        jnp.where(span_numbers[None, :] == order_table[:, None], counts_here[None, :], 0), axis=1
    )
    valid_mask = (
        jnp.arange(token_count, dtype=jnp.int32)[None, :] < counts_ordered[:, None]
    ).reshape(-1)
    keys_all = cache_rows[:, 0, :]
    values_all = cache_rows[:, 1, :]
    score_scale = 1.0 / math.sqrt(HD)

    def one_head(head_number):
        first_col = head_number * HD
        query_part = lax.dynamic_slice_in_dim(rotated_flat, first_col, HD, 1)
        key_part = lax.dynamic_slice_in_dim(keys_all, first_col, HD, 1)
        value_part = lax.dynamic_slice_in_dim(values_all, first_col, HD, 1)
        scores = (
            lax.dot_general(
                query_part, key_part, (((1,), (1,)), ((), ())), preferred_element_type=jnp.float32
            )
            * score_scale
        )
        masked = jnp.where(valid_mask[None, :], scores, -1e30)
        top_score = jnp.max(masked, axis=1, keepdims=True)
        weights = jnp.where(valid_mask[None, :], jnp.exp(masked - top_score), 0.0)
        totals = jnp.sum(weights, axis=1, keepdims=True)
        rounded = weights.astype(jnp.bfloat16)
        mixed = jnp.dot(rounded, value_part, preferred_element_type=jnp.float32)
        return (mixed / totals).astype(jnp.bfloat16)

    per_head = lax.map(one_head, jnp.arange(heads_here, dtype=jnp.int32))
    return jnp.transpose(per_head, (1, 0, 2)).reshape(token_count, width_here)


MESH = pl.DeviceIdType.MESH
LANES = 128
Z_ORDER = ((0, 1, 2, 3), (1, 0, 2, 3), (2, 3, 1, 0), (3, 2, 1, 0))
STEPS = ((0, 1), (1, 1), (0, 0), (2, 1), (1, 0), (3, 1), (2, 0), (3, 0))


def pick(index, values):
    out = jnp.int32(values[-1])
    for place in range(len(values) - 1):
        out = jnp.where(index == place, jnp.int32(values[place]), out)
    return out


def project_kernel(
    lat_ref, w_ref, shift_ref, scale_ref, gain_ref, cache_ref, counts_ref, group_ref,
    o_ref,
    lat, wbuf, acc, part, mean_s, rstd_s, cos_s, sin_s, rot, sq,
    cache, kv_own, kv_all, query, mixed, top, result,
    cache_sem, o_send, o_recv,
    lat_sem, w_local, w_recv, w_sendy, w_sendr, w_sendl,
    sq_recv, sq_send, q_send, q_recv, kv_recv, kv_y, kv_z, kv_relay, kv_sib,
):
    tile = lax.axis_index("tile")
    head = lax.axis_index("head")
    z, y = tile // 2, tile % 2
    core = head % 2
    zlow = z % 2
    tile_y = z * 2 + (1 - y)
    head_sib = head - core + (1 - core)
    zpair = z - zlow + (1 - zlow)
    tile_zp = zpair * 2 + y
    own = zlow * 2 + y
    own_y = zlow * 2 + (1 - y)
    far = (1 - zlow) * 2 + y
    far_y = (1 - zlow) * 2 + (1 - y)
    rows = lat.shape[0]
    depth = w_ref.shape[0]
    is_main = core == y
    not_main = core != y
    heads_here = acc.shape[1] // LANES

    def remote(src, dst, ssem, rsem, tile_to, head_to):
        return pltpu.make_async_remote_copy(
            src_ref=src, dst_ref=dst, send_sem=ssem, recv_sem=rsem,
            device_id=(tile_to, head_to), device_id_type=MESH,
        )

    def greet(tile_to, head_to):
        pl.semaphore_signal(
            barrier, inc=1, device_id=(tile_to, head_to), device_id_type=MESH
        )

    barrier = pltpu.get_barrier_semaphore()
    greet(tile_y, head)
    greet(tile_y, head_sib)
    for other in range(1, 4):
        greet(tile, (head + other) % 4)
    pl.when(z > 0)(lambda: greet(tile - 2, head))
    pl.when(z < 3)(lambda: greet(tile + 2, head))
    lat_copy = pltpu.make_async_copy(lat_ref, lat, lat_sem)
    lat_copy.start()
    cache_copy = pltpu.make_async_copy(cache_ref, cache, cache_sem)
    cache_copy.start()
    w_copy = pltpu.make_async_copy(w_ref, wbuf.at[tile], w_local)
    w_copy.start()
    pl.semaphore_wait(barrier, 5 + pick(z, (1, 2, 2, 1)))

    def send_y(zk):
        slot = zk * 2 + y
        return remote(wbuf.at[slot], wbuf.at[slot], w_sendy.at[zk], w_recv.at[slot], tile_y, head)

    def send_right(zk):
        slot = zk * 2 + y
        return remote(wbuf.at[slot], wbuf.at[slot], w_sendr.at[zk], w_recv.at[slot], tile + 2, head)

    def send_left(zk):
        slot = zk * 2 + y
        return remote(wbuf.at[slot], wbuf.at[slot], w_sendl.at[zk], w_recv.at[slot], tile - 2, head)

    def forward(zk):
        pl.when(jnp.logical_and(zk <= z, z < 3))(lambda: send_right(zk).start())
        pl.when(jnp.logical_and(zk >= z, z > 0))(lambda: send_left(zk).start())
        send_y(zk).start()

    def kv_to_y(i):
        return remote(
            kv_own.at[i], kv_all.at[i, own], kv_y.at[i], kv_recv.at[i, own], tile_y, head
        )

    def kv_slot(i, slot, ssem, tile_to, head_to):
        ref = kv_all.at[i, slot]
        return remote(ref, ref, ssem, kv_recv.at[i, slot], tile_to, head_to)

    def kv_to_z(i):
        return kv_slot(i, own, kv_z.at[i], tile_zp, head)

    def kv_to_relay(i):
        return kv_slot(i, own_y, kv_relay.at[i], tile_zp, head)

    def kv_to_sib(i, slot):
        return kv_slot(i, slot, kv_sib.at[i, slot], tile, head_sib)

    def kv_wait(i, slot):
        kv_to_sib(i, slot).wait_recv()

    w_copy.wait()
    forward(z)
    lat_copy.wait()

    part[...] = jnp.zeros_like(part)
    acc[:, :LANES] = jnp.zeros_like(part)

    def columns(i):
        return pl.ds(pl.multiple_of(i * LANES, LANES), LANES)

    @pl.loop(0, D // LANES)
    def _(i):
        x = lat[:, columns(i)].astype(jnp.float32)
        part[...] += x
        acc[:, :LANES] += x * x

    mean = jnp.sum(part[...], axis=1, keepdims=True) / D
    var = jnp.sum(acc[:, :LANES], axis=1, keepdims=True) / D - mean * mean
    mean_s[...] = jnp.broadcast_to(mean, mean_s.shape)
    rstd_s[...] = jnp.broadcast_to(lax.rsqrt(var + norm_eps), rstd_s.shape)

    @pl.loop(0, D // LANES)
    def _(i):
        x = lat[:, columns(i)].astype(jnp.float32)
        normed = (x - mean_s[...]) * rstd_s[...] * (1.0 + scale_ref[:, columns(i)])
        lat[:, columns(i)] = (normed + shift_ref[:, columns(i)]).astype(jnp.bfloat16)

    cache_copy.wait()

    @pl.when(is_main)
    def _():
        kv_all[0, own] = cache[:, 0, :]
        kv_all[1, own] = cache[:, 1, :]

    @pl.when(not_main)
    def _():
        kv_own[0] = cache[:, 0, :]
        kv_own[1] = cache[:, 1, :]

    lane = lax.broadcasted_iota(jnp.int32, (1, LANES), 1)
    pair = lane // 2
    space_pairs = HD // 6
    time_pairs = HD // 2 - 2 * space_pairs
    in_time = pair < time_pairs
    in_height = pair < time_pairs + space_pairs
    offset = jnp.where(
        in_time, pair, jnp.where(in_height, pair - time_pairs, pair - time_pairs - space_pairs)
    )
    extent = jnp.where(in_time, jnp.float32(time_pairs), jnp.float32(space_pairs))
    theta = jnp.exp(-math.log(10000.0) * offset.astype(jnp.float32) / extent)
    token = (
        own * rows + lax.broadcasted_iota(jnp.int32, (rows, LANES), 0)
    ).astype(jnp.float32)
    frame = jnp.floor((token + 0.5) * (1.0 / (GH * GW)))
    in_frame = token - frame * (GH * GW)
    height = jnp.floor((in_frame + 0.5) * (1.0 / GW))
    width = in_frame - height * GW
    time = (group_ref[0] * FRAMES).astype(jnp.float32) + frame
    position = jnp.where(in_time, time, jnp.where(in_height, height, width))
    angle = position * theta
    even = lane % 2 == 0
    cos_s[...] = jnp.cos(angle)
    sine = jnp.sin(angle)
    sin_s[...] = jnp.where(even, -sine, sine)

    acc[...] = jnp.zeros_like(acc)

    @pl.loop(0, 8)
    def _(e):
        k = pick(e, [s[0] for s in STEPS])
        along_z = pick(e, [s[1] for s in STEPS])
        zk = jnp.where(
            z == 0, pick(k, Z_ORDER[0]),
            jnp.where(z == 1, pick(k, Z_ORDER[1]),
                      jnp.where(z == 2, pick(k, Z_ORDER[2]), pick(k, Z_ORDER[3]))),
        )
        slot = zk * 2 + jnp.where(along_z == 1, y, 1 - y)

        @pl.when(e > 0)
        def _():
            remote(
                wbuf.at[slot], wbuf.at[slot], w_sendy.at[zk], w_recv.at[slot], tile_y, head
            ).wait_recv()

        @pl.when(jnp.logical_and(e > 0, along_z == 1))
        def _():
            forward(zk)

        @pl.when(jnp.logical_and(e == 5, is_main))
        def _():
            for i in range(2):
                kv_to_z(i).start()
                kv_to_sib(i, own).start()

        @pl.when(jnp.logical_and(e == 7, not_main))
        def _():
            for i in range(2):
                kv_to_y(i).start()

        cols = pl.ds(pl.multiple_of(slot * depth, LANES), depth)
        acc[...] += jnp.dot(lat[:, cols], wbuf[slot], preferred_element_type=jnp.float32)

    total = jnp.zeros((rows, LANES), jnp.float32)
    for h in range(heads_here):
        x = acc[:, h * LANES:(h + 1) * LANES]
        total = total + x * x
    part[...] = total
    sq[head] = lax.dot_general(
        jnp.ones((8, LANES), jnp.float32), part[...], (((1,), (1,)), ((), ())),
        preferred_element_type=jnp.float32, precision=lax.Precision.HIGHEST,
    )

    def sq_copy(other, slot):
        return remote(
            sq.at[slot], sq.at[slot], sq_send.at[other - 1], sq_recv.at[slot],
            tile, (head + other) % 4,
        )

    for other in range(1, 4):
        sq_copy(other, head).start()
    for other in range(1, 4):
        sq_copy(other, (head + other) % 4).wait_recv()
    for other in range(1, 4):
        sq_copy(other, head).wait_send()
    summed = sq[0] + sq[1] + sq[2] + sq[3]
    first = (lax.broadcasted_iota(jnp.int32, (8, LANES), 0) == 0).astype(jnp.float32)
    spread = lax.dot_general(
        summed, first, (((0,), (0,)), ((), ())),
        preferred_element_type=jnp.float32, precision=lax.Precision.HIGHEST,
    )
    rstd_s[...] = lax.rsqrt(spread / (HEADS * HD) + norm_eps)
    for h in range(heads_here):
        cut = slice(h * LANES, (h + 1) * LANES)
        x = acc[:, cut] * rstd_s[...] * gain_ref[:, cut]
        turned = jnp.where(
            even, pltpu.roll(x, LANES - 1, 1), pltpu.roll(x, 1, 1)
        )
        rot[:, cut] = (x * cos_s[...] + turned * sin_s[...]).astype(jnp.bfloat16)

    def q_out():
        return remote(rot, query, q_send, q_recv, tile_y, head_sib)

    pl.when(not_main)(lambda: q_out().start())

    @pl.when(is_main)
    def _():
        query[...] = rot[...]
        kv_wait(0, own_y)
        kv_to_relay(0).start()
        kv_to_sib(0, own_y).start()

    @pl.when(not_main)
    def _():
        q_out().wait_send()
        q_out().wait_recv()
        for i in range(2):
            kv_wait(i, own)

    factor = math.log2(math.e) / math.sqrt(HD)
    clip_first = tile // 4 * 4
    kv_lane = lax.broadcasted_iota(jnp.int32, (rows, LANES), 1)
    kv_row = lax.broadcasted_iota(jnp.int32, (rows, LANES), 0)
    mark = jnp.where(kv_lane == 0, 1.0, 0.0).astype(jnp.bfloat16)
    ones = jnp.ones((rows, LANES), jnp.bfloat16)
    top[...] = jnp.full(top.shape, -1e30, jnp.float32)
    mixed[...] = jnp.zeros_like(mixed)

    def o_out(h):
        cut = slice(h * LANES, (h + 1) * LANES)
        return remote(
            result.at[:, cut], o_ref.at[:, cut], o_send.at[h], o_recv.at[h], tile_y, head_sib
        )

    def o_stay(h):
        cut = slice(h * LANES, (h + 1) * LANES)
        return pltpu.make_async_copy(result.at[:, cut], o_ref.at[:, cut], o_recv.at[h])

    def attend_tile(slot, last):
        invalid = jnp.logical_and(kv_row >= counts_ref[clip_first + slot], kv_lane == 0)
        bias = jnp.where(invalid, -1e30, 0.0).astype(jnp.bfloat16)

        def score(h):
            cut = slice(h * LANES, (h + 1) * LANES)
            return lax.dot_general(
                jnp.concatenate([query[:, cut], mark], axis=1),
                jnp.concatenate([kv_all[0, slot, :, cut], bias], axis=1),
                (((1,), (1,)), ((), ())), preferred_element_type=jnp.float32,
            )

        following = score(0)
        for h in range(heads_here):
            cut = slice(h * LANES, (h + 1) * LANES)
            scores = following
            if h + 1 < heads_here:
                following = score(h + 1)
            before = top[:, h:h + 1]
            now = jnp.maximum(before, jnp.max(scores, axis=1, keepdims=True))
            weights = jnp.exp2((scores - now) * factor).astype(jnp.bfloat16)
            wide = slice(2 * h * LANES, 2 * (h + 1) * LANES)
            value = mixed[:, wide] * jnp.exp2((before - now) * factor) + jnp.dot(
                weights, jnp.concatenate([kv_all[1, slot, :, cut], ones], axis=1),
                preferred_element_type=jnp.float32,
            )
            if last:
                result[:, cut] = (value[:, :LANES] / value[:, LANES:]).astype(jnp.bfloat16)
                pl.when(not_main)(lambda: o_out(h).start())
                pl.when(is_main)(lambda: o_stay(h).start())
            else:
                top[:, h:h + 1] = now
                mixed[:, wide] = value

    @pl.loop(0, 3)
    def _(t):
        @pl.when(jnp.logical_and(t == 1, is_main))
        def _():
            kv_wait(1, own_y)
            kv_to_relay(1).start()
            kv_to_sib(1, own_y).start()

        @pl.when(jnp.logical_and(t == 2, is_main))
        def _():
            for i in range(2):
                kv_wait(i, far)
                kv_to_sib(i, far).start()

        slot = jnp.where(t == 0, own, jnp.where(t == 1, own_y, far))

        @pl.when(jnp.logical_and(t > 0, not_main))
        def _():
            for i in range(2):
                kv_wait(i, slot)

        attend_tile(slot, False)

    for i in range(2):
        kv_wait(i, far_y)
        pl.when(is_main)(lambda: kv_to_sib(i, far_y).start())
    attend_tile(far_y, True)

    @pl.when(is_main)
    def _():
        for i in range(2):
            kv_to_z(i).wait_send()
            kv_to_relay(i).wait_send()
            for slot in (own, own_y, far, far_y):
                kv_to_sib(i, slot).wait_send()
        for h in range(heads_here):
            o_stay(h).wait()

    @pl.when(not_main)
    def _():
        for i in range(2):
            kv_to_y(i).wait_send()
        for h in range(heads_here):
            o_out(h).wait_send()
            o_out(h).wait_recv()

    for zk in range(4):
        send_y(zk).wait_send()
        pl.when(jnp.logical_and(zk <= z, z < 3))(lambda: send_right(zk).wait_send())
        pl.when(jnp.logical_and(zk >= z, z > 0))(lambda: send_left(zk).wait_send())


def project(
    latents, query_weight, mod_shift, mod_scale, query_gain, cache_blocks, block_counts, group_index
):
    rows, width = latents.shape[0], query_weight.shape[1]
    any_spec = pl.BlockSpec(memory_space=pl.ANY)
    vmem = pl.BlockSpec(memory_space=pltpu.VMEM)
    smem = pl.BlockSpec(memory_space=pltpu.SMEM)
    dma = pltpu.SemaphoreType.DMA
    wide = pltpu.VMEM((rows, LANES), jnp.float32)
    return pl.pallas_call(
        project_kernel,
        out_shape=jax.ShapeDtypeStruct((rows, width), jnp.bfloat16),
        in_specs=[any_spec, any_spec, vmem, vmem, vmem, any_spec, smem, smem],
        out_specs=any_spec,
        scratch_shapes=[
            pltpu.VMEM((rows, D), jnp.bfloat16),
            pltpu.VMEM((8,) + query_weight.shape, jnp.bfloat16),
            pltpu.VMEM((rows, width), jnp.float32),
            wide, wide, wide, wide, wide,
            pltpu.VMEM((rows, width), jnp.bfloat16),
            pltpu.VMEM((4, 8, rows), jnp.float32),
            pltpu.VMEM(cache_blocks.shape, jnp.bfloat16),
            pltpu.VMEM((2, rows, width), jnp.bfloat16),
            pltpu.VMEM((2, 4, rows, width), jnp.bfloat16),
            pltpu.VMEM((rows, width), jnp.bfloat16),
            pltpu.VMEM((rows, 2 * width), jnp.float32),
            wide,
            pltpu.VMEM((rows, width), jnp.bfloat16),
            dma(()), dma((width // LANES,)), dma((width // LANES,)),
            dma(()), dma(()), dma((8,)), dma((4,)), dma((4,)), dma((4,)),
            dma((4,)), dma((3,)), dma(()), dma(()),
            dma((2, 4)), dma((2,)), dma((2,)), dma((2,)), dma((2, 4)),
        ],
        compiler_params=pltpu.CompilerParams(
            collective_id=0, has_side_effects=True, vmem_limit_bytes=63 * 2**20
        ),
    )(
        latents, query_weight, mod_shift[None], mod_scale[None], query_gain[None],
        cache_blocks, block_counts, group_index,
    )


def solution(mesh):
    in_specs = (
        P("tile", None),
        P("tile", "head"),
        P(),
        P(),
        P("head"),
        P("tile", None, "head"),
        P(),
        P(),
    )
    out_specs = P("tile", "head")
    square = mesh.shape["tile"] == 8 and mesh.shape["head"] == 4
    return jax.shard_map(
        project if square else per_device, mesh=mesh,
        in_specs=in_specs,
        out_specs=out_specs,
        check_vma=False,
    )
```
